32 devices in a mesh: row: 8 (over y, x, core), col: 4 (over z).
Axes of the slice: x: 2, y: 2, z: 4, core: 2. Of those that a mesh axis runs over, the one named last changes fastest.
Arguments:
- features: float32 [16384, 256], P(('col', 'row')), may hold values from -6 to 6
- weight_matrix: float32 [256, 256], replicated, may hold values from -0.375 to 0.375
- cotangent: float32 [16384, 256], P(('row', 'col')), may hold values from -6 to 6
- block_rows: int32 [8, 4, 96], P('row', 'col'), may hold values from 0 to 15
- block_cols: int32 [8, 4, 96], P('row', 'col'), may hold values from 0 to 31
- blocks: float32 [8, 4, 96, 128, 128], P('row', 'col'), may hold values from -0.109375 to 0.109375
Outputs:
- hidden: float32 [16384, 256], P(('row', 'col'))
- weight_grad: float32 [256, 256], replicated
- feature_grad: float32 [16384, 256], P(('col', 'row'))
The draws below stay inside these ranges and needn't reach their ends.
All inputs are finite; a program needn't handle non-finite values.
Results may differ from the reference program's by a relative error of at most 0.0001.
Values sent between devices are 32-bit elements; how exact they have to be, the bound alone decides.
No kernel may reach another device: no remote copies, remote signals or barrier semaphores. Data moves between devices by JAX's collectives and lax.ppermute only.
A program may use at most 128 MiB of HBM per device.

```python
import math
import jax
import jax.numpy as jnp
import numpy as np
from jax import lax

F = 256
BS = 128
NB = 96
NODES = 16384
RB = 16
CB = 32
N_ROW = 8
N_COL = 4


def set_ends(array, key, smallest, top_value):
    spot = [jax.random.randint(jax.random.fold_in(key, axis), (), 0, length) for axis, length in enumerate(array.shape)]
    longest = array.shape.index(max(array.shape))
    next_to = spot[:longest] + [(spot[longest] + 1) % array.shape[longest]] + spot[longest + 1:]
    return array.at[tuple(spot)].set(smallest).at[tuple(next_to)].set(top_value)


def steps_of(rng, dims, split, smallest, high):
    loudness = 1.0
    for dim, parts in split:
        draws = jax.random.uniform(jax.random.fold_in(jax.random.fold_in(rng, 6), dim), (parts,), jnp.float32, smallest / len(split), high / len(split))
        loudness = loudness * jnp.repeat(jnp.exp(draws), dims[dim] // parts).reshape((-1,) + (1,) * (len(dims) - 1 - dim))
    return loudness


def rank_table(count, slope):
    weights = [(1 << 20) // math.isqrt(rank ** slope) + 1 for rank in range(1, count + 1)]
    scale = 1 + sum(weights) // (1 << 30)
    return np.cumsum(np.array([max(1, weight // scale) for weight in weights]))


def ranked_ids(key, extent, number_of, skew):
    grid = rank_table(number_of, skew)
    ticket = jax.random.randint(jax.random.fold_in(key, 1), extent, 0, int(grid[number_of - 1]))
    standing = jnp.searchsorted(jnp.asarray(grid, jnp.int32), ticket, side="right")
    return jax.random.permutation(jax.random.fold_in(key, 2), number_of)[standing].astype(jnp.int32)


def bell_draw(key, dims, scale, most, pieces=(), held_as=jnp.bfloat16):
    array = jax.random.normal(key, dims, jnp.float32) * scale
    if len(pieces) > 0:
        array = steps_of(key, dims, pieces, -0.22, 0.18) * array
    return jnp.clip(array, min=-most, max=most).astype(held_as)


def setup_inputs(seed: int = 0) -> dict:
    streams_of = jax.random.split(jax.random.key(seed), 7)
    features = bell_draw(streams_of[0], (NODES, F), 1.0, 6.0, ((0, 32),), jnp.float32)
    weight_matrix = bell_draw(streams_of[1], (F, F), F ** -0.5, 0.375, (), jnp.float32)
    cotangent = bell_draw(streams_of[2], (NODES, F), 1.0, 6.0, ((0, 32),), jnp.float32)
    block_rows = set_ends(ranked_ids(streams_of[3], (N_ROW, N_COL, NB), RB, 2), jax.random.fold_in(streams_of[3], 3), 0, RB - 1).astype(jnp.int32)
    block_cols = set_ends(jax.random.randint(streams_of[4], (N_ROW, N_COL, NB), 0, CB), jax.random.fold_in(streams_of[4], 1), 0, CB - 1).astype(jnp.int32)
    blocks = bell_draw(streams_of[5], (N_ROW, N_COL, NB, BS, BS), (BS * NB * N_COL // RB) ** -0.5, 0.109375, ((0, 8), (1, 4)), jnp.float32)
    return dict(features=features, weight_matrix=weight_matrix, cotangent=cotangent, block_rows=block_rows, block_cols=block_cols, blocks=blocks)


def activate(pre, cotangent):
    sigmoid_v = 1.0 / (1.0 + jnp.exp(-pre))
    return (pre * sigmoid_v, cotangent * sigmoid_v * (1.0 + pre * (1.0 - sigmoid_v)))

def reference(features, weight_matrix, cotangent, block_rows, block_cols, blocks):
    high = lax.Precision.HIGHEST
    total_blocks = NODES // BS
    row_base = (jnp.arange(N_ROW, dtype=jnp.int32) * RB)[:, None, None]
    col_base = (jnp.arange(N_COL, dtype=jnp.int32) * CB)[None, :, None]
    global_rows = (block_rows + row_base).reshape(N_ROW * N_COL, NB).astype(jnp.int32)
    global_cols = (block_cols + col_base).reshape(N_ROW * N_COL, NB).astype(jnp.int32)
    tile_values = blocks.reshape(N_ROW * N_COL, NB, BS, BS)

    def spread(source, take, put, form):
        source_blocks = source.reshape(total_blocks, BS, F)

        def step(total, item):
            take_ids, put_ids, values = item
            products = jnp.einsum(form, values, source_blocks[take_ids], precision=high)
            return (total.at[put_ids].add(products), None)
        start = jnp.zeros((total_blocks, BS, F), jnp.float32)
        total, unused = lax.scan(step, start, (take, put, tile_values))
        return total.reshape(NODES, F)
    aggregated = spread(features, global_cols, global_rows, 'kij,kjf->kif')
    pre = jnp.dot(aggregated, weight_matrix, precision=high)
    hidden, dpre = activate(pre, cotangent)
    weight_grad = jnp.dot(aggregated.T, dpre, precision=high) / jnp.sqrt(jnp.float32(NODES))
    back = jnp.dot(dpre, weight_matrix.T, precision=high)
    feature_grad = spread(back, global_rows, global_cols, 'kji,kjf->kif')
    return (hidden, weight_grad, feature_grad)
```

```python
import functools

import jax
import jax.numpy as jnp
from jax import lax
from jax.experimental import pallas as pl
from jax.experimental.pallas import tpu as pltpu
from jax.sharding import PartitionSpec as P

VMEM_LIMIT = 52 * 1024 * 1024

OUTER = ((0, 1), (1, 0), (2, 3), (3, 2))
MIDDLE = ((1, 2), (2, 1))
INWARD = ((0, 1), (3, 2))
OUTWARD = ((1, 0), (2, 3))
ACROSS = ((0, 2), (1, 3), (2, 0), (3, 1))


def two_terms(x):
    high = x.astype(jnp.bfloat16)
    low = (x - high.astype(jnp.float32)).astype(jnp.bfloat16)
    return high, low


def dot_terms(left, right, dims):
    left_high, left_low = two_terms(left)
    right_high, right_low = two_terms(right)
    dot = functools.partial(
        lax.dot_general, dimension_numbers=(dims, ((), ())), preferred_element_type=jnp.float32
    )
    return dot(left_high, right_high) + (dot(left_high, right_low) + dot(left_low, right_high))


def row_slot(block, place, per, swap):
    group = (block // per) ^ place[1]
    if swap:
        group = group ^ (place[2] & (2 * (group & 1)))
    return group * per + block % per


def col_slot(block, place, per):
    return ((block // per) ^ place[0]) * per + block % per


def spmm_kernel(count_in, count_out, per_step, per, transposed, place, rows_ref, cols_ref, values_ref, *refs):
    pieces, outs = refs[:count_in], refs[count_in : count_in + count_out]
    source, total = refs[count_in + count_out :]
    size = values_ref.shape[-1]
    width = total.shape[-1]
    step = pl.program_id(0)

    @pl.when(step == 0)
    def _():
        slot = 0
        for piece in pieces:
            for block in range(piece.shape[0] // size):
                high, low = two_terms(piece[pl.ds(block * size, size), :])
                both = jnp.concatenate([high, low], axis=1)
                source[slot, pl.ds(0, size), :] = both
                source[slot, pl.ds(size, size), :] = both
                slot += 1
        total[...] = jnp.zeros_like(total)

    for k in range(per_step):
        row, col = rows_ref[step * per_step + k], cols_ref[step * per_step + k]
        if transposed:
            take, put = row_slot(row, place, per, False), col_slot(col, place, per)
        else:
            take, put = col_slot(col, place, per), row_slot(row, place, per, True)
        axis = 0 if transposed else 1
        left = jnp.concatenate(two_terms(values_ref[k]), axis=axis)
        product = lax.dot_general(
            left, source[take], (((axis,), (0,)), ((), ())), preferred_element_type=jnp.float32
        )
        total[put] += product[:, :width] + product[:, width:]

    @pl.when(step == pl.num_programs(0) - 1)
    def _():
        slot = 0
        for out in outs:
            for block in range(out.shape[0] // size):
                out[pl.ds(block * size, size), :] = total[slot]
                slot += 1


def spmm(place, rows, cols, values, pieces, out_rows, per, transposed):
    count, size = values.shape[0], values.shape[-1]
    width = pieces[0].shape[1]
    per_step = next(p for p in (8, 4, 2, 1) if count % p == 0)
    in_blocks = sum(p.shape[0] for p in pieces) // size
    out_blocks = sum(out_rows) // size
    whole = lambda rows: pl.BlockSpec((rows, width), lambda i, *_: (0, 0))
    return pl.pallas_call(
        functools.partial(spmm_kernel, len(pieces), len(out_rows), per_step, per, transposed),
        out_shape=[jax.ShapeDtypeStruct((rows, width), jnp.float32) for rows in out_rows],
        grid_spec=pltpu.PrefetchScalarGridSpec(
            num_scalar_prefetch=3,
            grid=(count // per_step,),
            in_specs=[pl.BlockSpec((per_step, size, size), lambda i, *_: (i, 0, 0))]
            + [whole(p.shape[0]) for p in pieces],
            out_specs=[whole(rows) for rows in out_rows],
            scratch_shapes=[
                pltpu.VMEM((in_blocks, 2 * size, 2 * width), jnp.bfloat16),
                pltpu.VMEM((out_blocks, size, width), jnp.float32),
            ],
        ),
        compiler_params=pltpu.CompilerParams(vmem_limit_bytes=VMEM_LIMIT),
        cost_estimate=pl.CostEstimate(
            flops=8 * count * size * size * width,
            bytes_accessed=4 * (values.size + (in_blocks + out_blocks) * size * width),
            transcendentals=0,
        ),
    )(place, rows, cols, values, *pieces)


def dense_kernel(count_parts, place, *refs):
    halves = []
    for half in range(2):
        parts = refs[half * count_parts : (half + 1) * count_parts]
        rows = parts[0][...]
        if count_parts > 1:
            rows = rows + jnp.where(place[2] != 0, parts[1][...], 0.0)
            for part in parts[2:]:
                rows = rows + part[...]
        halves.append(rows)
    cotangent, weight, hidden, back_first, back_second, grad_out = refs[2 * count_parts :]
    width = back_first.shape[1]
    rows = jnp.concatenate(halves, axis=1)
    pre = dot_terms(rows, weight[...], ((1,), (0,)))
    sigmoid_v = 1.0 / (1.0 + jnp.exp(-pre))
    hidden[...] = pre * sigmoid_v
    dpre = cotangent[...] * sigmoid_v * (1.0 + pre * (1.0 - sigmoid_v))
    back = dot_terms(dpre, weight[...], ((1,), (1,)))
    back_first[...] = back[:, :width]
    back_second[...] = back[:, width:]
    grad_out[...] = dot_terms(rows, dpre, ((0,), (0,)))


def dense(place, parts, cotangent, weight):
    rows, width = cotangent.shape
    vmem = pl.BlockSpec(memory_space=pltpu.VMEM)
    return pl.pallas_call(
        functools.partial(dense_kernel, len(parts) // 2),
        in_specs=[pl.BlockSpec(memory_space=pltpu.SMEM)] + [vmem] * (len(parts) + 2),
        out_shape=[
            jax.ShapeDtypeStruct((rows, width), jnp.float32),
            jax.ShapeDtypeStruct((rows, width // 2), jnp.float32),
            jax.ShapeDtypeStruct((rows, width // 2), jnp.float32),
            jax.ShapeDtypeStruct((width, width), jnp.float32),
        ],
        compiler_params=pltpu.CompilerParams(vmem_limit_bytes=VMEM_LIMIT),
        cost_estimate=pl.CostEstimate(
            flops=18 * rows * width * width,
            bytes_accessed=4 * (len(parts) // 2 + 3) * rows * width + 8 * width * width,
            transcendentals=rows * width,
        ),
    )(place, *parts, cotangent, weight)


def along_row(x, bit):
    return lax.ppermute(x, "row", [(i, i ^ bit) for i in range(lax.axis_size("row"))])


def along_col(x, pairs):
    return lax.ppermute(x, "col", pairs)


def plane_gather(own):
    mine = [own] + [along_row(own, bit) for bit in (2, 4, 6)]
    other = [along_row(piece, 1) for piece in mine]
    return [piece for pair in zip(mine, other) for piece in pair]


def plane_reduce(pieces):
    sums = [pieces[p] + along_row(pieces[p + 1], 1) for p in (0, 2, 4, 6)]
    return sums[0] + along_row(sums[1], 2) + along_row(sums[2], 4) + along_row(sums[3], 6)


def line_reduce(slots, edge):
    own, outer, across, inner = slots
    near = along_col(outer, OUTER)
    inward = along_col(inner, INWARD)
    middle = along_col(inner, MIDDLE)
    far = along_col(across + jnp.where(edge, 0.0, near), ACROSS)
    return [own, near, inward, middle, far]


def line_gather(own):
    across = along_col(own, ACROSS)
    near = along_col(own, OUTER)
    middle = along_col(own, MIDDLE)
    outward = along_col(across, OUTWARD)
    return [own, near, across, middle + outward]


def grad_sum(grad):
    me = lax.axis_index("row")
    rows = grad.shape[0]
    for bit in (1, 2, 4):
        rows //= 2
        upper = (me // bit) % 2
        keep = lax.dynamic_slice_in_dim(grad, upper * rows, rows, 0)
        send = lax.dynamic_slice_in_dim(grad, (1 - upper) * rows, rows, 0)
        grad = keep + along_row(send, bit)
    grad = grad + along_col(grad, OUTER)
    grad = grad + along_col(grad, ACROSS)
    for bit in (4, 2, 1):
        upper = (me // bit) % 2
        other = along_row(grad, bit)
        grad = jnp.where(upper == 1, jnp.concatenate([other, grad], axis=0), jnp.concatenate([grad, other], axis=0))
    return grad


def shards(features, weight_matrix, cotangent, block_rows, block_cols, blocks):
    tile = (block_rows[0, 0], block_cols[0, 0], blocks[0, 0])
    size = blocks.shape[-1]
    rows_dev, width = features.shape
    per = rows_dev // size
    count_row, count_col = lax.axis_size("row"), lax.axis_size("col")
    total_nodes = rows_dev * count_row * count_col
    me_row, me_col = lax.axis_index("row"), lax.axis_index("col")
    half = width // 2
    features = (features[:, :half], features[:, half:])

    if (count_row, count_col) == (8, 4):
        edge = (me_col == 0) | (me_col == 3)
        place = jnp.stack([me_row, me_col, jnp.where(edge, 2, 0)]).astype(jnp.int32)
        parts = []
        for own in features:
            slots = spmm(place, *tile, plane_gather(own), [rows_dev] * 4, per, False)
            parts += line_reduce(slots, edge)
        hidden, *backs, grad = dense(place, parts, cotangent, weight_matrix)
        grads = []
        for back in backs:
            sums = spmm(place, *tile, line_gather(back), [rows_dev] * 8, per, True)
            grads.append(plane_reduce(sums))
        grad = grad_sum(grad)
    else:
        place = jnp.zeros((3,), jnp.int32)
        parts = []
        for own in features:
            gathered = lax.all_gather(own, "row", axis=0, tiled=True)
            (partial,) = spmm(place, *tile, [gathered], [rows_dev * count_col], per, False)
            parts.append(lax.psum_scatter(partial, "col", scatter_dimension=0, tiled=True))
        hidden, *backs, grad = dense(place, parts, cotangent, weight_matrix)
        grads = []
        for back in backs:
            gathered = lax.all_gather(back, "col", axis=0, tiled=True)
            (partial,) = spmm(place, *tile, [gathered], [rows_dev * count_row], per, True)
            grads.append(lax.psum_scatter(partial, "row", scatter_dimension=0, tiled=True))
        grad = lax.psum(grad, ("row", "col"))

    weight_grad = grad / jnp.sqrt(jnp.float32(total_nodes))
    return (hidden, weight_grad, jnp.concatenate(grads, axis=1))


def solution(mesh):
    in_specs = (
        P(("col", "row"), None),
        P(),
        P(("row", "col"), None),
        P("row", "col", None),
        P("row", "col", None),
        P("row", "col", None, None, None),
    )
    out_specs = (P(("row", "col"), None), P(), P(("col", "row"), None))
    return jax.shard_map(shards, mesh=mesh, in_specs=in_specs, out_specs=out_specs, check_vma=False)
```

```python
import functools

import jax
import jax.numpy as jnp
from jax import lax
from jax.experimental import pallas as pl
from jax.experimental.pallas import tpu as pltpu
from jax.sharding import PartitionSpec as P

VMEM_LIMIT = 52 * 1024 * 1024

OUTER = ((0, 1), (1, 0), (2, 3), (3, 2))
MIDDLE = ((1, 2), (2, 1))
INWARD = ((0, 1), (3, 2))
OUTWARD = ((1, 0), (2, 3))
ACROSS = ((0, 2), (1, 3), (2, 0), (3, 1))
REVERSED = ((0, 3), (1, 2), (2, 1), (3, 0))
ENDS_ACROSS = ((0, 2), (3, 1), (1, 0), (2, 3))
ENDS_INWARD = ((2, 0), (1, 3), (0, 1), (3, 2))


def two_terms(x):
    high = x.astype(jnp.bfloat16)
    low = (x - high.astype(jnp.float32)).astype(jnp.bfloat16)
    return high, low


def dot_terms(left, right, dims):
    left_high, left_low = two_terms(left)
    right_high, right_low = two_terms(right)
    dot = functools.partial(
        lax.dot_general, dimension_numbers=(dims, ((), ())), preferred_element_type=jnp.float32
    )
    return dot(left_high, right_high) + (dot(left_high, right_low) + dot(left_low, right_high))


def row_slot(block, place, per, gathered):
    group = (block // per) ^ place[1]
    if gathered:
        group = group ^ (place[3] * ((group ^ (group >> 1)) & 1))
    else:
        group = group ^ (place[2] * (group & 1))
    return group * per + block % per


def col_slot(block, place, per):
    return ((block // per) ^ place[0]) * per + block % per


def spmm_kernel(groups, only, has_base, count_out, steps, unroll, per, transposed, ids, values_hbm, *refs):
    count_in = sum(groups)
    pieces, refs = refs[:count_in], refs[count_in:]
    base, refs = (refs[0], refs[1:]) if has_base else (None, refs)
    outs, refs = refs[:count_out], refs[count_out:]
    landed, source, total, values, picked, value_sem, piece_sem, base_sem, out_sem = refs
    count, size = values.shape[0], values.shape[-1]
    halves = source.shape[1]
    width = total.shape[-1] // halves
    each = count // steps
    zero_slot = source.shape[0] - 1

    def value_copy(step):
        part = pl.ds(step * each, each)
        return pltpu.make_async_copy(values_hbm.at[part], values.at[part], value_sem.at[step])

    copies, start = [], 0
    for index, piece in enumerate(pieces):
        part = pl.ds(start, piece.shape[0])
        copies.append(pltpu.make_async_copy(piece, landed.at[part], piece_sem.at[index]))
        start += piece.shape[0]
    for copy in copies:
        copy.start()
    for step in range(steps):
        value_copy(step).start()
    if has_base:
        base_copy = pltpu.make_async_copy(base, total, base_sem.at[0])
        base_copy.start()
    else:
        total[...] = jnp.zeros_like(total)

    def slots_of(index):
        row, col = ids[4 + index], ids[4 + count + index]
        if transposed:
            return row_slot(row, ids, per, True), col_slot(col, ids, per)
        return col_slot(col, ids, per), row_slot(row, ids, per, False)

    if only is not None:
        source[zero_slot] = jnp.zeros_like(source[zero_slot])

        def pick(index, found):
            take, _ = slots_of(index)
            picked[found] = index
            return found + jnp.where((take >= only[0]) & (take < only[1]), 1, 0)

        found = lax.fori_loop(0, count, pick, 0)

    first, slot, start = 0, 0, 0
    for group in groups:
        rows = pieces[first].shape[0]
        for copy in copies[first : first + group]:
            copy.wait()
        for block in range(rows // size):
            terms = [landed[pl.ds(start + m * rows + block * size, size), :] for m in range(group)]
            whole = sum(terms[1:], terms[0])
            for half in range(halves):
                both = jnp.concatenate(two_terms(whole[:, half * width : (half + 1) * width]), axis=1)
                source[slot, half, pl.ds(0, size), :] = both
                source[slot, half, pl.ds(size, size), :] = both
            slot += 1
        first, start = first + group, start + group * rows

    def add_block(index, take, put):
        axis = 0 if transposed else 1
        left = jnp.concatenate(two_terms(values[index]), axis=axis)
        rows = pl.ds(pl.multiple_of(put * size, size), size)
        for half in range(halves):
            product = lax.dot_general(
                left, source[take, half], (((axis,), (0,)), ((), ())), preferred_element_type=jnp.float32
            )
            columns = pl.ds(half * width, width)
            total[rows, columns] += product[:, :width] + product[:, width:]

    if only is None:
        for step in range(steps):
            value_copy(step).wait()

            @pl.loop(0, each // unroll)
            def _(index):
                for k in range(unroll):
                    add_block(step * each + index * unroll + k, *slots_of(step * each + index * unroll + k))

    else:
        for step in range(steps):
            value_copy(step).wait()
        if has_base:
            base_copy.wait()

        def add_picked(step, carry):
            for k in range(unroll):
                place = step * unroll + k
                index = jnp.where(place < found, picked[jnp.minimum(place, count)], 0)
                take, put = slots_of(index)
                add_block(index, jnp.where(place < found, take - only[0], zero_slot), put)
            return carry

        lax.fori_loop(0, (found + unroll - 1) // unroll, add_picked, 0)

    copies, start = [], 0
    for index, out in enumerate(outs):
        part = pl.ds(start, out.shape[0])
        copies.append(pltpu.make_async_copy(total.at[part], out, out_sem.at[index]))
        copies[-1].start()
        start += out.shape[0]
    for copy in copies:
        copy.wait()


def spmm(ids, values, groups, out_rows, per, transposed, only=None, base=None):
    pieces = [piece for group in groups for piece in group]
    count, size = values.shape[0], values.shape[-1]
    width = pieces[0].shape[1]
    halves = max(1, width // size)
    unroll = next(p for p in ((32, 16, 8, 4, 2, 1) if only is None else (8, 4, 2, 1)) if count % p == 0)
    steps = count // unroll if only is None else 1
    in_rows = sum(group[0].shape[0] for group in groups)
    smem, anywhere = pl.BlockSpec(memory_space=pltpu.SMEM), pl.BlockSpec(memory_space=pl.ANY)
    bases = [] if base is None else [base]
    return pl.pallas_call(
        functools.partial(
            spmm_kernel,
            [len(group) for group in groups],
            only,
            base is not None,
            len(out_rows),
            steps,
            unroll,
            per,
            transposed,
        ),
        out_shape=[jax.ShapeDtypeStruct((rows, width), jnp.float32) for rows in out_rows],
        in_specs=[smem] + [anywhere] * (1 + len(pieces) + len(bases)),
        out_specs=[anywhere] * len(out_rows),
        scratch_shapes=[
            pltpu.VMEM((sum(piece.shape[0] for piece in pieces), width), jnp.float32),
            pltpu.VMEM((in_rows // size + 1, halves, 2 * size, 2 * (width // halves)), jnp.bfloat16),
            pltpu.VMEM((sum(out_rows), width), jnp.float32),
            pltpu.VMEM(values.shape, jnp.float32),
            pltpu.SMEM((count + 1,), jnp.int32),
            pltpu.SemaphoreType.DMA((steps,)),
            pltpu.SemaphoreType.DMA((len(pieces),)),
            pltpu.SemaphoreType.DMA((1,)),
            pltpu.SemaphoreType.DMA((len(out_rows),)),
        ],
        compiler_params=pltpu.CompilerParams(vmem_limit_bytes=VMEM_LIMIT),
        cost_estimate=pl.CostEstimate(
            flops=8 * count * size * size * width,
            bytes_accessed=4 * (values.size + (in_rows + sum(out_rows)) * width),
            transcendentals=0,
        ),
    )(ids, values, *pieces, *bases)


def dense_kernel(count_parts, ids, *refs):
    halves = []
    for half in range(2):
        parts = refs[half * count_parts : (half + 1) * count_parts]
        rows = parts[0][...]
        if count_parts > 1:
            rows = rows + jnp.where(ids[2] != 0, parts[1][...], 0.0)
            for part in parts[2:]:
                rows = rows + part[...]
        halves.append(rows)
    cotangent, weight, hidden, back, grad_out = refs[2 * count_parts :]
    rows = jnp.concatenate(halves, axis=1)
    pre = dot_terms(rows, weight[...], ((1,), (0,)))
    sigmoid_v = 1.0 / (1.0 + jnp.exp(-pre))
    hidden[...] = pre * sigmoid_v
    dpre = cotangent[...] * sigmoid_v * (1.0 + pre * (1.0 - sigmoid_v))
    back[...] = dot_terms(dpre, weight[...], ((1,), (1,)))
    grad_out[...] = dot_terms(rows, dpre, ((0,), (0,)))


def dense(ids, parts, cotangent, weight):
    rows, width = cotangent.shape
    vmem = pl.BlockSpec(memory_space=pltpu.VMEM)
    return pl.pallas_call(
        functools.partial(dense_kernel, len(parts) // 2),
        in_specs=[pl.BlockSpec(memory_space=pltpu.SMEM)] + [vmem] * (len(parts) + 2),
        out_shape=[
            jax.ShapeDtypeStruct((rows, width), jnp.float32),
            jax.ShapeDtypeStruct((rows, width), jnp.float32),
            jax.ShapeDtypeStruct((width, width), jnp.float32),
        ],
        compiler_params=pltpu.CompilerParams(vmem_limit_bytes=VMEM_LIMIT),
        cost_estimate=pl.CostEstimate(
            flops=1000,
            bytes_accessed=1000,
            transcendentals=0,
        ),
    )(ids, *parts, cotangent, weight)


def along_row(x, bit):
    return lax.ppermute(x, "row", [(i, i ^ bit) for i in range(lax.axis_size("row"))])


def along_col(x, pairs):
    return lax.ppermute(x, "col", pairs)


def after(x, *others):
    return lax.optimization_barrier((x, *others))[0]


def both_cores(mine, *others):
    return [piece for own in mine for piece in (own, along_row(after(own, *others), 1))]


def plane_exchange(pieces, *others):
    return [pieces[p] + along_row(after(pieces[p + 1], *others), 1) for p in (0, 2, 4, 6)]


def line_reduce(slots, edge, earlier):
    own, outer, across, inner = slots
    outer, middle = after(outer, *earlier), after(inner, *earlier)
    near, middle = along_col(outer, OUTER), along_col(middle, MIDDLE)
    far = along_col(after(across + jnp.where(edge, 0.0, near), middle), ACROSS)
    inward = along_col(after(inner, near, middle), INWARD)
    return [own, near, middle, far, inward]


def plane_sum(grad):
    upper = lax.axis_index("row") % 2
    rows = grad.shape[0] // 2
    keep = lax.dynamic_slice_in_dim(grad, upper * rows, rows, 0)
    send = lax.dynamic_slice_in_dim(grad, (1 - upper) * rows, rows, 0)
    grad = keep + along_row(send, 1)
    grad = grad + along_row(grad, 2)
    return grad + along_row(grad, 4)


def both_halves(grad, *others):
    other = along_row(after(grad, *others), 1)
    upper = lax.axis_index("row") % 2
    return jnp.where(upper == 1, jnp.concatenate([other, grad], axis=0), jnp.concatenate([grad, other], axis=0))


def shards(features, weight_matrix, cotangent, block_rows, block_cols, blocks):
    values = blocks[0, 0]
    size = blocks.shape[-1]
    rows_dev, width = features.shape
    per = rows_dev // size
    count_row, count_col = lax.axis_size("row"), lax.axis_size("col")
    total_nodes = rows_dev * count_row * count_col
    me_row, me_col = lax.axis_index("row"), lax.axis_index("col")
    half = width // 2
    features = (features[:, :half], features[:, half:])

    if (count_row, count_col) == (8, 4):
        edge = (me_col == 0) | (me_col == 3)
        place = jnp.stack([me_row, me_col, jnp.where(edge, 2, 0), jnp.where(edge, 0, 3)]).astype(jnp.int32)
        ids = jnp.concatenate([place, block_rows[0, 0], block_cols[0, 0]])
        first, second = features
        diagonal = along_row(first, 6)
        mine = [first, along_row(first, 2), along_row(first, 4), diagonal]
        pieces = both_cores(mine)
        slots = spmm(ids, values, [[p] for p in pieces], [rows_dev] * 4, per, False)
        second = after(second, diagonal)
        mine = [second, along_row(second, 2), along_row(second, 4), along_row(second, 6)]
        terms = line_reduce(slots, edge, [])
        pieces = both_cores(mine, slots[0])
        pieces[0] = after(pieces[0], *terms[1:3])
        slots = spmm(ids, values, [[p] for p in pieces], [rows_dev] * 4, per, False)
        terms += line_reduce(slots, edge, terms[3:5])
        hidden, back, grad = dense(ids, terms, cotangent, weight_matrix)

        ends_across = along_col(back, ENDS_ACROSS)
        later = after(back, ends_across)
        ends_inward, middle = along_col(later, ENDS_INWARD), along_col(later, MIDDLE)
        outward = along_col(ends_across, OUTWARD)
        near_part = spmm(
            ids, values, [[back], [ends_across]], [rows_dev * count_row], per, True, (0, 2 * per)
        )[0]
        grad = plane_sum(after(grad, ends_across))
        groups = [[after(ends_inward, grad)], [middle, outward]]
        sums = plane_exchange(
            spmm(ids, values, groups, [rows_dev] * 8, per, True, (2 * per, 4 * per), near_part)
        )
        others = [along_row(sums[k], 2 * k) for k in (3, 1, 2)]
        feature_grad = sums[0] + others[0] + others[1] + others[2]
        grad = after(grad, sums[3])
        grad = both_halves(grad + along_col(grad, OUTER) + along_col(grad, ACROSS) + along_col(grad, REVERSED), *others)
    else:
        place = jnp.zeros((4,), jnp.int32)
        ids = jnp.concatenate([place, block_rows[0, 0], block_cols[0, 0]])
        parts = []
        for own in features:
            gathered = lax.all_gather(own, "row", axis=0, tiled=True)
            (partial,) = spmm(ids, values, [[gathered]], [rows_dev * count_col], per, False)
            parts.append(lax.psum_scatter(partial, "col", scatter_dimension=0, tiled=True))
        hidden, back, grad = dense(ids, parts, cotangent, weight_matrix)
        gathered = lax.all_gather(back, "col", axis=0, tiled=True)
        (partial,) = spmm(ids, values, [[gathered]], [rows_dev * count_row], per, True)
        feature_grad = lax.psum_scatter(partial, "row", scatter_dimension=0, tiled=True)
        grad = lax.psum(grad, ("row", "col"))

    weight_grad = grad / jnp.sqrt(jnp.float32(total_nodes))
    return (hidden, weight_grad, feature_grad)


def solution(mesh):
    in_specs = (
        P(("col", "row"), None),
        P(),
        P(("row", "col"), None),
        P("row", "col", None),
        P("row", "col", None),
        P("row", "col", None, None, None),
    )
    out_specs = (P(("row", "col"), None), P(), P(("col", "row"), None))
    return jax.shard_map(shards, mesh=mesh, in_specs=in_specs, out_specs=out_specs, check_vma=False)
```

```python
import functools

import jax
import jax.numpy as jnp
from jax import lax
from jax.experimental import pallas as pl
from jax.experimental.pallas import tpu as pltpu
from jax.sharding import PartitionSpec as P

VMEM_LIMIT = 52 * 1024 * 1024

OUTER = ((0, 1), (1, 0), (2, 3), (3, 2))
MIDDLE = ((1, 2), (2, 1))
INWARD = ((0, 1), (3, 2))
OUTWARD = ((1, 0), (2, 3))
ACROSS = ((0, 2), (1, 3), (2, 0), (3, 1))
ENDS_ACROSS = ((0, 2), (3, 1), (1, 0), (2, 3))
ENDS_INWARD = ((2, 0), (1, 3), (0, 1), (3, 2))


def two_terms(x):
    high = x.astype(jnp.bfloat16)
    low = (x - high.astype(jnp.float32)).astype(jnp.bfloat16)
    return high, low


def dot_terms(left, right, dims):
    left_high, left_low = two_terms(left)
    right_high, right_low = two_terms(right)
    dot = functools.partial(
        lax.dot_general, dimension_numbers=(dims, ((), ())), preferred_element_type=jnp.float32
    )
    return dot(left_high, right_high) + (dot(left_high, right_low) + dot(left_low, right_high))


def split_index(block, per):
    if per & (per - 1) == 0:
        return block >> (per.bit_length() - 1), block & (per - 1)
    return block // per, block % per


def row_slot(block, place, per, gathered):
    chunk, inside = split_index(block, per)
    group = chunk ^ place[1]
    if gathered:
        group = group ^ (place[3] * ((group ^ (group >> 1)) & 1))
    else:
        group = group ^ (place[2] * (group & 1))
    return group * per + inside


def col_slot(block, place, per):
    chunk, inside = split_index(block, per)
    return (chunk ^ place[0]) * per + inside


def spmm_kernel(groups, only, has_base, count_out, steps, unroll, per, transposed, ids, values_hbm, *refs):
    count_in = sum(groups)
    pieces, refs = refs[:count_in], refs[count_in:]
    (base, listed), refs = (refs[:2], refs[2:]) if has_base else ((None, None), refs)
    outs, refs = refs[:count_out], refs[count_out:]
    if only is not None and not has_base:
        listed, refs = refs[0], refs[1:]
    landed, source, total, values, value_sem, piece_sem, base_sem, out_sem = refs
    count, size = values.shape[0], values.shape[-1]
    halves = source.shape[1]
    width = total.shape[-1] // halves
    each = count // steps
    zero_slot = source.shape[0] - 1

    def value_copy(step):
        part = pl.ds(step * each, each)
        return pltpu.make_async_copy(values_hbm.at[part], values.at[part], value_sem.at[step])

    copies, start = [], 0
    for index, piece in enumerate(pieces):
        part = pl.ds(start, piece.shape[0])
        copies.append(pltpu.make_async_copy(piece, landed.at[part], piece_sem.at[index]))
        start += piece.shape[0]
    if has_base:
        base_copy = pltpu.make_async_copy(base, total, base_sem.at[0])
        base_copy.start()
    for copy in copies:
        copy.start()
    if only is None:
        for step in range(steps):
            value_copy(step).start()
    if not has_base:
        total[...] = jnp.zeros_like(total)

    def slots_of(index):
        row, col = ids[4 + index], ids[4 + count + index]
        if transposed:
            return row_slot(row, ids, per, True), col_slot(col, ids, per)
        return col_slot(col, ids, per), row_slot(row, ids, per, False)

    if only is not None:
        source[zero_slot] = jnp.zeros_like(source[zero_slot])

        if not has_base:

            def pick(index, found):
                take, _ = slots_of(index)
                wanted = (take >= only[0]) & (take < only[1])
                listed[jnp.where(wanted, found, count - 1 - index + found)] = index
                return found + wanted.astype(jnp.int32)

            listed[count] = lax.fori_loop(0, count, pick, 0)

        found = count - listed[count] if has_base else listed[count]

        def picked(place):
            return listed[count - 1 - place if has_base else place]

        def picked_copy(place):
            return pltpu.make_async_copy(values_hbm.at[picked(place)], values.at[place], value_sem.at[place])

        def start_copy(place, carry):
            picked_copy(place).start()
            return carry

        lax.fori_loop(0, found, start_copy, 0)

    first, slot, start = 0, 0, 0
    for group in groups:
        rows = pieces[first].shape[0]
        for copy in copies[first : first + group]:
            copy.wait()
        for block in range(rows // size):
            terms = [landed[pl.ds(start + m * rows + block * size, size), :] for m in range(group)]
            whole = sum(terms[1:], terms[0])
            for half in range(halves):
                both = jnp.concatenate(two_terms(whole[:, half * width : (half + 1) * width]), axis=1)
                source[slot, half, pl.ds(0, size), :] = both
                source[slot, half, pl.ds(size, size), :] = both
            slot += 1
        first, start = first + group, start + group * rows

    def add_block(place, take, put):
        axis = 0 if transposed else 1
        left = jnp.concatenate(two_terms(values[place]), axis=axis)
        rows = pl.ds(pl.multiple_of(put * size, size), size)
        for half in range(halves):
            product = lax.dot_general(
                left, source[take, half], (((axis,), (0,)), ((), ())), preferred_element_type=jnp.float32
            )
            columns = pl.ds(half * width, width)
            total[rows, columns] += product[:, :width] + product[:, width:]

    if only is None:
        for step in range(steps):
            value_copy(step).wait()

            @pl.loop(0, each // unroll)
            def _(index):
                for k in range(unroll):
                    add_block(step * each + index * unroll + k, *slots_of(step * each + index * unroll + k))

    else:
        if has_base:
            base_copy.wait()

        def add_picked(step, carry):
            for k in range(unroll):
                place = step * unroll + k

                @pl.when(place < found)
                def _():
                    picked_copy(place).wait()

            for k in range(unroll):
                place = step * unroll + k
                inside = place < found
                place = jnp.where(inside, place, 0)
                take, put = slots_of(picked(place))
                add_block(place, jnp.where(inside, take - only[0], zero_slot), put)
            return carry

        lax.fori_loop(0, (found + unroll - 1) // unroll, add_picked, 0)

    copies, start = [], 0
    for index, out in enumerate(outs):
        part = pl.ds(start, out.shape[0])
        copies.append(pltpu.make_async_copy(total.at[part], out, out_sem.at[index]))
        copies[-1].start()
        start += out.shape[0]
    for copy in copies:
        copy.wait()


def spmm(ids, values, groups, out_rows, per, transposed, only=None, rest=()):
    pieces = [piece for group in groups for piece in group]
    count, size = values.shape[0], values.shape[-1]
    width = pieces[0].shape[1]
    halves = max(1, width // size)
    unroll = next(p for p in ((32, 16, 8, 4, 2, 1) if only is None else (8, 4, 2, 1)) if count % p == 0)
    steps = count // unroll if only is None else 1
    in_rows = sum(group[0].shape[0] for group in groups)
    smem, anywhere = pl.BlockSpec(memory_space=pltpu.SMEM), pl.BlockSpec(memory_space=pl.ANY)
    lists = only is not None and not rest
    return pl.pallas_call(
        functools.partial(
            spmm_kernel,
            [len(group) for group in groups],
            only,
            bool(rest),
            len(out_rows),
            steps,
            unroll,
            per,
            transposed,
        ),
        out_shape=[jax.ShapeDtypeStruct((rows, width), jnp.float32) for rows in out_rows]
        + [jax.ShapeDtypeStruct((count + 1,), jnp.int32)] * lists,
        in_specs=[smem] + [anywhere] * (1 + len(pieces)) + [anywhere, smem][: len(rest)],
        out_specs=[anywhere] * len(out_rows) + [smem] * lists,
        scratch_shapes=[
            pltpu.VMEM((sum(piece.shape[0] for piece in pieces), width), jnp.float32),
            pltpu.VMEM((in_rows // size + 1, halves, 2 * size, 2 * (width // halves)), jnp.bfloat16),
            pltpu.VMEM((sum(out_rows), width), jnp.float32),
            pltpu.VMEM(values.shape, jnp.float32),
            pltpu.SemaphoreType.DMA((steps if only is None else count,)),
            pltpu.SemaphoreType.DMA((len(pieces),)),
            pltpu.SemaphoreType.DMA((1,)),
            pltpu.SemaphoreType.DMA((len(out_rows),)),
        ],
        compiler_params=pltpu.CompilerParams(vmem_limit_bytes=VMEM_LIMIT),
        cost_estimate=pl.CostEstimate(
            flops=8 * count * size * size * width,
            bytes_accessed=4 * (values.size + (in_rows + sum(out_rows)) * width),
            transcendentals=0,
        ),
    )(ids, values, *pieces, *rest)


def dense_kernel(count_parts, ids, *refs):
    halves = []
    for half in range(2):
        parts = refs[half * count_parts : (half + 1) * count_parts]
        rows = parts[0][...]
        if count_parts > 1:
            rows = rows + jnp.where(ids[2] != 0, parts[1][...], 0.0)
            for part in parts[2:]:
                rows = rows + part[...]
        halves.append(rows)
    cotangent, weight, hidden, back, grad_out = refs[2 * count_parts :]
    rows = jnp.concatenate(halves, axis=1)
    pre = dot_terms(rows, weight[...], ((1,), (0,)))
    sigmoid_v = 1.0 / (1.0 + jnp.exp(-pre))
    hidden[...] = pre * sigmoid_v
    dpre = cotangent[...] * sigmoid_v * (1.0 + pre * (1.0 - sigmoid_v))
    back[...] = dot_terms(dpre, weight[...], ((1,), (1,)))
    grad_out[...] = dot_terms(rows, dpre, ((0,), (0,)))


def dense(ids, parts, cotangent, weight):
    rows, width = cotangent.shape
    vmem = pl.BlockSpec(memory_space=pltpu.VMEM)
    return pl.pallas_call(
        functools.partial(dense_kernel, len(parts) // 2),
        in_specs=[pl.BlockSpec(memory_space=pltpu.SMEM)] + [vmem] * (len(parts) + 2),
        out_shape=[
            jax.ShapeDtypeStruct((rows, width), jnp.float32),
            jax.ShapeDtypeStruct((rows, width), jnp.float32),
            jax.ShapeDtypeStruct((width, width), jnp.float32),
        ],
        compiler_params=pltpu.CompilerParams(vmem_limit_bytes=VMEM_LIMIT),
        cost_estimate=pl.CostEstimate(
            flops=1000,
            bytes_accessed=1000,
            transcendentals=0,
        ),
    )(ids, *parts, cotangent, weight)


def along_row(x, bit):
    return lax.ppermute(x, "row", [(i, i ^ bit) for i in range(lax.axis_size("row"))])


def along_col(x, pairs):
    return lax.ppermute(x, "col", pairs)


def after(x, *others):
    return lax.optimization_barrier((x, *others))[0]


def both_cores(mine, *others):
    return [piece for own in mine for piece in (own, along_row(after(own, *others), 1))]


def plane_exchange(pieces, *others):
    return [pieces[p] + along_row(after(pieces[p + 1], *others), 1) for p in (0, 2, 4, 6)]


def line_reduce(slots, edge, earlier):
    own, outer, across, inner = slots
    outer, middle = after(outer, *earlier), after(inner, *earlier)
    near, middle = along_col(outer, OUTER), along_col(middle, MIDDLE)
    far = along_col(after(across + jnp.where(edge, 0.0, near), middle), ACROSS)
    inward = along_col(after(inner, near, middle), INWARD)
    return [own, near, middle, far, inward]


def core_half(grad):
    upper = lax.axis_index("row") % 2
    rows = grad.shape[0] // 2
    keep = lax.dynamic_slice_in_dim(grad, upper * rows, rows, 0)
    send = lax.dynamic_slice_in_dim(grad, (1 - upper) * rows, rows, 0)
    return keep + along_row(send, 1)


def both_halves(grad):
    other = along_row(grad, 1)
    upper = lax.axis_index("row") % 2
    return jnp.where(upper == 1, jnp.concatenate([other, grad], axis=0), jnp.concatenate([grad, other], axis=0))


def shards(features, weight_matrix, cotangent, block_rows, block_cols, blocks):
    values = blocks[0, 0]
    size = blocks.shape[-1]
    rows_dev, width = features.shape
    per = rows_dev // size
    count_row, count_col = lax.axis_size("row"), lax.axis_size("col")
    total_nodes = rows_dev * count_row * count_col
    me_row, me_col = lax.axis_index("row"), lax.axis_index("col")
    half = width // 2
    features = (features[:, :half], features[:, half:])

    if (count_row, count_col) == (8, 4):
        edge = (me_col == 0) | (me_col == 3)
        place = jnp.stack([me_row, me_col, jnp.where(edge, 2, 0), jnp.where(edge, 0, 3)]).astype(jnp.int32)
        ids = jnp.concatenate([place, block_rows[0, 0], block_cols[0, 0]])
        first, second = features
        diagonal = along_row(first, 6)
        mine = [first, along_row(first, 2), along_row(first, 4), diagonal]
        pieces = both_cores(mine)
        slots = spmm(ids, values, [[p] for p in pieces], [rows_dev] * 4, per, False)
        second = after(second, diagonal)
        mine = [second, along_row(second, 2), along_row(second, 4), along_row(second, 6)]
        terms = line_reduce(slots, edge, [])
        pieces = both_cores(mine, slots[0])
        pieces[0] = after(pieces[0], *terms[1:3])
        slots = spmm(ids, values, [[p] for p in pieces], [rows_dev] * 4, per, False)
        terms += line_reduce(slots, edge, terms[3:5])
        hidden, back, grad = dense(ids, terms, cotangent, weight_matrix)

        ends_across = along_col(back, ENDS_ACROSS)
        later = after(back, ends_across)
        ends_inward, middle = along_col(later, ENDS_INWARD), along_col(later, MIDDLE)
        outward = along_col(ends_across, OUTWARD)
        rest = spmm(ids, values, [[back], [ends_across]], [rows_dev * count_row], per, True, (0, 2 * per))
        grad = core_half(grad)
        grads = [along_row(after(grad, ends_across), bit) for bit in (2, 4, 6)]
        groups = [[after(ends_inward, *grads)], [middle, outward]]
        sums = plane_exchange(
            spmm(ids, values, groups, [rows_dev] * 8, per, True, (2 * per, 4 * per), rest)
        )
        grad = after(grad + grads[0] + grads[1] + grads[2], ends_inward, middle, outward)
        grad = grad + along_col(grad, OUTER)
        upper, lower = sums[3][: rows_dev // 2], sums[3][rows_dev // 2 :]
        upper, lower = after(along_row(upper, 2), grad), along_row(lower, 4)
        others = [
            along_row(sums[1] + jnp.pad(lower, ((rows_dev // 2, 0), (0, 0))), 2),
            along_row(sums[2] + jnp.pad(upper, ((0, rows_dev // 2), (0, 0))), 4),
        ]
        feature_grad = sums[0] + others[0] + others[1]
        grad = both_halves(grad + along_col(grad, ACROSS))
    else:
        place = jnp.zeros((4,), jnp.int32)
        ids = jnp.concatenate([place, block_rows[0, 0], block_cols[0, 0]])
        parts = []
        for own in features:
            gathered = lax.all_gather(own, "row", axis=0, tiled=True)
            (partial,) = spmm(ids, values, [[gathered]], [rows_dev * count_col], per, False)
            parts.append(lax.psum_scatter(partial, "col", scatter_dimension=0, tiled=True))
        hidden, back, grad = dense(ids, parts, cotangent, weight_matrix)
        gathered = lax.all_gather(back, "col", axis=0, tiled=True)
        (partial,) = spmm(ids, values, [[gathered]], [rows_dev * count_row], per, True)
        feature_grad = lax.psum_scatter(partial, "row", scatter_dimension=0, tiled=True)
        grad = lax.psum(grad, ("row", "col"))

    weight_grad = grad / jnp.sqrt(jnp.float32(total_nodes))
    return (hidden, weight_grad, feature_grad)


def solution(mesh):
    in_specs = (
        P(("col", "row"), None),
        P(),
        P(("row", "col"), None),
        P("row", "col", None),
        P("row", "col", None),
        P("row", "col", None, None, None),
    )
    out_specs = (P(("row", "col"), None), P(), P(("col", "row"), None))
    return jax.shard_map(shards, mesh=mesh, in_specs=in_specs, out_specs=out_specs, check_vma=False)
```

```python
import functools
import math

import jax
import jax.numpy as jnp
from jax import lax
from jax.experimental import pallas as pl
from jax.experimental.pallas import tpu as pltpu
from jax.sharding import PartitionSpec as P

MIB = 1024 * 1024

OUTER = ((0, 1), (1, 0), (2, 3), (3, 2))
MIDDLE = ((1, 2), (2, 1))
INWARD = ((0, 1), (3, 2))
OUTWARD = ((1, 0), (2, 3))
ACROSS = ((0, 2), (1, 3), (2, 0), (3, 1))
ENDS_ACROSS = ((0, 2), (3, 1), (1, 0), (2, 3))
ENDS_INWARD = ((2, 0), (1, 3), (0, 1), (3, 2))


def two_terms(x):
    high = x.astype(jnp.bfloat16)
    low = (x - high.astype(jnp.float32)).astype(jnp.bfloat16)
    return high, low


def dot_terms(left, right, dims):
    left_high, left_low = two_terms(left)
    right_high, right_low = two_terms(right)
    dot = functools.partial(
        lax.dot_general, dimension_numbers=(dims, ((), ())), preferred_element_type=jnp.float32
    )
    return dot(left_high, right_high) + (dot(left_high, right_low) + dot(left_low, right_high))


def split_index(block, per):
    if per & (per - 1) == 0:
        return block >> (per.bit_length() - 1), block & (per - 1)
    return block // per, block % per


def row_slot(block, place, per, gathered):
    chunk, inside = split_index(block, per)
    group = chunk ^ place[1]
    if gathered:
        group = group ^ (place[3] * ((group ^ (group >> 1)) & 1))
    else:
        group = group ^ (place[2] * (group & 1))
    return group * per + inside


def col_slot(block, place, per):
    chunk, inside = split_index(block, per)
    return (chunk ^ place[0]) * per + inside


def spmm_kernel(groups, only, has_base, count_out, steps, unroll, per, transposed, ids, values_hbm, *refs):
    count_in = sum(groups)
    pieces, refs = refs[:count_in], refs[count_in:]
    (base, listed), refs = (refs[:2], refs[2:]) if has_base else ((None, None), refs)
    outs, refs = refs[:count_out], refs[count_out:]
    if only is not None and not has_base:
        listed, refs = refs[0], refs[1:]
    landed, source, total, values, value_sem, piece_sem, base_sem, out_sem = refs
    count, size = values.shape[0], values.shape[-1]
    halves = source.shape[1]
    width = total.shape[-1] // halves
    each = count // steps
    zero_slot = source.shape[0] - 1

    def value_copy(step):
        part = pl.ds(step * each, each)
        return pltpu.make_async_copy(values_hbm.at[part], values.at[part], value_sem.at[step])

    copies, start = [], 0
    for index, piece in enumerate(pieces):
        part = pl.ds(start, piece.shape[0])
        copies.append(pltpu.make_async_copy(piece, landed.at[part], piece_sem.at[index]))
        start += piece.shape[0]
    if has_base:
        base_copy = pltpu.make_async_copy(base, total, base_sem.at[0])
        base_copy.start()
    for copy in copies:
        copy.start()
    if only is None:
        for step in range(steps):
            value_copy(step).start()
    if not has_base:
        total[...] = jnp.zeros_like(total)

    def slots_of(index):
        row, col = ids[4 + index], ids[4 + count + index]
        if transposed:
            return row_slot(row, ids, per, True), col_slot(col, ids, per)
        return col_slot(col, ids, per), row_slot(row, ids, per, False)

    if only is not None:
        source[zero_slot] = jnp.zeros_like(source[zero_slot])

        if not has_base:

            def pick(index, found):
                take, _ = slots_of(index)
                wanted = (take >= only[0]) & (take < only[1])
                listed[jnp.where(wanted, found, count - 1 - index + found)] = index
                return found + wanted.astype(jnp.int32)

            listed[count] = lax.fori_loop(0, count, pick, 0)

        found = count - listed[count] if has_base else listed[count]

        def picked(place):
            return listed[count - 1 - place if has_base else place]

        def picked_copy(place):
            return pltpu.make_async_copy(values_hbm.at[picked(place)], values.at[place], value_sem.at[place])

        def start_copy(place, carry):
            picked_copy(place).start()
            return carry

        lax.fori_loop(0, found, start_copy, 0)

    first, slot, start = 0, 0, 0
    for group in groups:
        rows = pieces[first].shape[0]
        for copy in copies[first : first + group]:
            copy.wait()
        for block in range(rows // size):
            terms = [landed[pl.ds(start + m * rows + block * size, size), :] for m in range(group)]
            whole = sum(terms[1:], terms[0])
            for half in range(halves):
                both = jnp.concatenate(two_terms(whole[:, half * width : (half + 1) * width]), axis=1)
                source[slot, half, pl.ds(0, size), :] = both
                source[slot, half, pl.ds(size, size), :] = both
            slot += 1
        first, start = first + group, start + group * rows

    def add_block(place, take, put):
        axis = 0 if transposed else 1
        left = jnp.concatenate(two_terms(values[place]), axis=axis)
        rows = pl.ds(pl.multiple_of(put * size, size), size)
        for half in range(halves):
            product = lax.dot_general(
                left, source[take, half], (((axis,), (0,)), ((), ())), preferred_element_type=jnp.float32
            )
            columns = pl.ds(half * width, width)
            total[rows, columns] += product[:, :width] + product[:, width:]

    if only is None:
        for step in range(steps):
            value_copy(step).wait()

            @pl.loop(0, each // unroll)
            def _(index):
                for k in range(unroll):
                    add_block(step * each + index * unroll + k, *slots_of(step * each + index * unroll + k))

    else:
        if has_base:
            base_copy.wait()

        def add_picked(step, carry):
            for k in range(unroll):
                place = step * unroll + k

                @pl.when(place < found)
                def _():
                    picked_copy(place).wait()

            for k in range(unroll):
                place = step * unroll + k
                inside = place < found
                place = jnp.where(inside, place, 0)
                take, put = slots_of(picked(place))
                add_block(place, jnp.where(inside, take - only[0], zero_slot), put)
            return carry

        lax.fori_loop(0, (found + unroll - 1) // unroll, add_picked, 0)

    copies, start = [], 0
    for index, out in enumerate(outs):
        part = pl.ds(start, out.shape[0])
        copies.append(pltpu.make_async_copy(total.at[part], out, out_sem.at[index]))
        copies[-1].start()
        start += out.shape[0]
    for copy in copies:
        copy.wait()


def spmm(ids, values, groups, out_rows, per, transposed, only=None, rest=()):
    pieces = [piece for group in groups for piece in group]
    count, size = values.shape[0], values.shape[-1]
    width = pieces[0].shape[1]
    halves = max(1, width // size)
    unroll = next(p for p in ((32, 16, 8, 4, 2, 1) if only is None else (8, 4, 2, 1)) if count % p == 0)
    steps = count // unroll if only is None else 1
    in_rows = sum(group[0].shape[0] for group in groups)
    smem, anywhere = pl.BlockSpec(memory_space=pltpu.SMEM), pl.BlockSpec(memory_space=pl.ANY)
    lists = only is not None and not rest
    buffers = [
        pltpu.VMEM((sum(piece.shape[0] for piece in pieces), width), jnp.float32),
        pltpu.VMEM((in_rows // size + 1, halves, 2 * size, 2 * (width // halves)), jnp.bfloat16),
        pltpu.VMEM((sum(out_rows), width), jnp.float32),
        pltpu.VMEM(values.shape, jnp.float32),
    ]
    return pl.pallas_call(
        functools.partial(
            spmm_kernel,
            [len(group) for group in groups],
            only,
            bool(rest),
            len(out_rows),
            steps,
            unroll,
            per,
            transposed,
        ),
        out_shape=[jax.ShapeDtypeStruct((rows, width), jnp.float32) for rows in out_rows]
        + [jax.ShapeDtypeStruct((count + 1,), jnp.int32)] * lists,
        in_specs=[smem] + [anywhere] * (1 + len(pieces)) + [anywhere, smem][: len(rest)],
        out_specs=[anywhere] * len(out_rows) + [smem] * lists,
        scratch_shapes=buffers
        + [
            pltpu.SemaphoreType.DMA((steps if only is None else count,)),
            pltpu.SemaphoreType.DMA((len(pieces),)),
            pltpu.SemaphoreType.DMA((1,)),
            pltpu.SemaphoreType.DMA((len(out_rows),)),
        ],
        compiler_params=pltpu.CompilerParams(
            vmem_limit_bytes=40 * MIB
            if only
            else sum(math.prod(b.shape) * b.dtype.itemsize for b in buffers) + 4 * MIB
        ),
        cost_estimate=pl.CostEstimate(
            flops=8 * count * size * size * width,
            bytes_accessed=4 * (values.size + (in_rows + sum(out_rows)) * width),
            transcendentals=0,
        ),
    )(ids, values, *pieces, *rest)


def dense_kernel(count_parts, ids, *refs):
    halves = []
    for half in range(2):
        parts = refs[half * count_parts : (half + 1) * count_parts]
        rows = parts[0][...]
        if count_parts > 1:
            rows = rows + jnp.where(ids[2] != 0, parts[1][...], 0.0)
            for part in parts[2:]:
                rows = rows + part[...]
        halves.append(rows)
    cotangent, weight, hidden, back, grad_out = refs[2 * count_parts :]
    rows = jnp.concatenate(halves, axis=1)
    pre = dot_terms(rows, weight[...], ((1,), (0,)))
    sigmoid_v = 1.0 / (1.0 + jnp.exp(-pre))
    hidden[...] = pre * sigmoid_v
    dpre = cotangent[...] * sigmoid_v * (1.0 + pre * (1.0 - sigmoid_v))
    back[...] = dot_terms(dpre, weight[...], ((1,), (1,)))
    grad_out[...] = dot_terms(rows, dpre, ((0,), (0,)))


def dense(ids, parts, cotangent, weight):
    rows, width = cotangent.shape
    vmem = pl.BlockSpec(memory_space=pltpu.VMEM)
    return pl.pallas_call(
        functools.partial(dense_kernel, len(parts) // 2),
        in_specs=[pl.BlockSpec(memory_space=pltpu.SMEM)] + [vmem] * (len(parts) + 2),
        out_shape=[
            jax.ShapeDtypeStruct((rows, width), jnp.float32),
            jax.ShapeDtypeStruct((rows, width), jnp.float32),
            jax.ShapeDtypeStruct((width, width), jnp.float32),
        ],
        compiler_params=pltpu.CompilerParams(vmem_limit_bytes=20 * MIB),
        cost_estimate=pl.CostEstimate(
            flops=1000,
            bytes_accessed=1000,
            transcendentals=0,
        ),
    )(ids, *parts, cotangent, weight)


def along_row(x, bit):
    return lax.ppermute(x, "row", [(i, i ^ bit) for i in range(lax.axis_size("row"))])


def along_col(x, pairs):
    return lax.ppermute(x, "col", pairs)


def after(x, *others):
    return lax.optimization_barrier((x, *others))[0]


def both_cores(mine, *others):
    return [piece for own in mine for piece in (own, along_row(after(own, *others), 1))]


def plane_exchange(pieces, *others):
    return [pieces[p] + along_row(after(pieces[p + 1], *others), 1) for p in (0, 2, 4, 6)]


def line_reduce(slots, edge, earlier):
    own, outer, across, inner = slots
    outer, middle = after(outer, *earlier), after(inner, *earlier)
    near, middle = along_col(outer, OUTER), along_col(middle, MIDDLE)
    far = along_col(after(across + jnp.where(edge, 0.0, near), middle), ACROSS)
    inward = along_col(after(inner, near, middle), INWARD)
    return [own, near, middle, far, inward]


def core_half(grad):
    upper = lax.axis_index("row") % 2
    rows = grad.shape[0] // 2
    keep = lax.dynamic_slice_in_dim(grad, upper * rows, rows, 0)
    send = lax.dynamic_slice_in_dim(grad, (1 - upper) * rows, rows, 0)
    return keep + along_row(send, 1)


def both_halves(grad):
    other = along_row(grad, 1)
    upper = lax.axis_index("row") % 2
    return jnp.where(upper == 1, jnp.concatenate([other, grad], axis=0), jnp.concatenate([grad, other], axis=0))


def shards(features, weight_matrix, cotangent, block_rows, block_cols, blocks):
    values = blocks[0, 0]
    size = blocks.shape[-1]
    rows_dev, width = features.shape
    per = rows_dev // size
    count_row, count_col = lax.axis_size("row"), lax.axis_size("col")
    total_nodes = rows_dev * count_row * count_col
    me_row, me_col = lax.axis_index("row"), lax.axis_index("col")
    half = width // 2
    features = (features[:, :half], features[:, half:])

    if (count_row, count_col) == (8, 4):
        edge = (me_col == 0) | (me_col == 3)
        place = jnp.stack([me_row, me_col, jnp.where(edge, 2, 0), jnp.where(edge, 0, 3)]).astype(jnp.int32)
        ids = jnp.concatenate([place, block_rows[0, 0], block_cols[0, 0]])
        first, second = features
        diagonal = along_row(first, 6)
        mine = [first, along_row(first, 2), along_row(first, 4), diagonal]
        pieces = both_cores(mine, ids)
        slots = spmm(ids, values, [[p] for p in pieces], [rows_dev] * 4, per, False)
        second = after(second, diagonal)
        mine = [second, along_row(second, 2), along_row(second, 4), along_row(second, 6)]
        terms = line_reduce(slots, edge, [])
        pieces = both_cores(mine, slots[0])
        pieces[0] = after(pieces[0], *terms[1:3])
        slots = spmm(ids, values, [[p] for p in pieces], [rows_dev] * 4, per, False)
        terms += line_reduce(slots, edge, terms[3:5])
        hidden, back, grad = dense(ids, terms, cotangent, weight_matrix)

        ends_across = along_col(back, ENDS_ACROSS)
        later = after(back, ends_across)
        ends_inward, middle = along_col(later, ENDS_INWARD), along_col(later, MIDDLE)
        outward = along_col(ends_across, OUTWARD)
        rest = spmm(ids, values, [[back], [ends_across]], [rows_dev * count_row], per, True, (0, 2 * per))
        grad = core_half(grad)
        grads = [along_row(after(grad, ends_across), bit) for bit in (2, 4, 6)]
        groups = [[after(ends_inward, *grads)], [middle, outward]]
        sums = plane_exchange(
            spmm(ids, values, groups, [rows_dev] * 8, per, True, (2 * per, 4 * per), rest)
        )
        grad = after(grad + grads[0] + grads[1] + grads[2], ends_inward, middle, outward)
        grad = grad + along_col(grad, OUTER)
        upper, lower = sums[3][: rows_dev // 2], sums[3][rows_dev // 2 :]
        upper, lower = after(along_row(upper, 2), grad), along_row(lower, 4)
        others = [
            along_row(sums[1] + jnp.pad(lower, ((rows_dev // 2, 0), (0, 0))), 2),
            along_row(sums[2] + jnp.pad(upper, ((0, rows_dev // 2), (0, 0))), 4),
        ]
        feature_grad = sums[0] + others[0] + others[1]
        grad = both_halves(grad + along_col(grad, ACROSS))
    else:
        place = jnp.zeros((4,), jnp.int32)
        ids = jnp.concatenate([place, block_rows[0, 0], block_cols[0, 0]])
        parts = []
        for own in features:
            gathered = lax.all_gather(own, "row", axis=0, tiled=True)
            (partial,) = spmm(ids, values, [[gathered]], [rows_dev * count_col], per, False)
            parts.append(lax.psum_scatter(partial, "col", scatter_dimension=0, tiled=True))
        hidden, back, grad = dense(ids, parts, cotangent, weight_matrix)
        gathered = lax.all_gather(back, "col", axis=0, tiled=True)
        (partial,) = spmm(ids, values, [[gathered]], [rows_dev * count_row], per, True)
        feature_grad = lax.psum_scatter(partial, "row", scatter_dimension=0, tiled=True)
        grad = lax.psum(grad, ("row", "col"))

    weight_grad = grad / jnp.sqrt(jnp.float32(total_nodes))
    return (hidden, weight_grad, feature_grad)


def solution(mesh):
    in_specs = (
        P(("col", "row"), None),
        P(),
        P(("row", "col"), None),
        P("row", "col", None),
        P("row", "col", None),
        P("row", "col", None, None, None),
    )
    out_specs = (P(("row", "col"), None), P(), P(("col", "row"), None))
    return jax.shard_map(shards, mesh=mesh, in_specs=in_specs, out_specs=out_specs, check_vma=False)
```

```python
import functools
import math

import jax
import jax.numpy as jnp
from jax import lax
from jax.experimental import pallas as pl
from jax.experimental.pallas import tpu as pltpu
from jax.sharding import PartitionSpec as P

MIB = 1024 * 1024

OUTER = ((0, 1), (1, 0), (2, 3), (3, 2))
MIDDLE = ((1, 2), (2, 1))
INWARD = ((0, 1), (3, 2))
OUTWARD = ((1, 0), (2, 3))
ACROSS = ((0, 2), (1, 3), (2, 0), (3, 1))
ENDS_ACROSS = ((0, 2), (3, 1), (1, 0), (2, 3))
ENDS_INWARD = ((2, 0), (1, 3), (0, 1), (3, 2))


def two_terms(x):
    high = x.astype(jnp.bfloat16)
    low = (x - high.astype(jnp.float32)).astype(jnp.bfloat16)
    return high, low


def dot_terms(left, right, dims):
    left_high, left_low = two_terms(left)
    right_high, right_low = two_terms(right)
    dot = functools.partial(
        lax.dot_general, dimension_numbers=(dims, ((), ())), preferred_element_type=jnp.float32
    )
    return dot(left_high, right_high) + (dot(left_high, right_low) + dot(left_low, right_high))


def split_index(block, per):
    if per & (per - 1) == 0:
        return block >> (per.bit_length() - 1), block & (per - 1)
    return block // per, block % per


def row_slot(block, place, per, gathered):
    chunk, inside = split_index(block, per)
    group = chunk ^ place[1]
    if gathered:
        group = group ^ (place[3] * ((group ^ (group >> 1)) & 1))
    else:
        group = group ^ (place[2] * (group & 1))
    return group * per + inside


def col_slot(block, place, per):
    chunk, inside = split_index(block, per)
    return (chunk ^ place[0]) * per + inside


def spmm_kernel(groups, only, has_base, count_out, steps, unroll, per, transposed, ids, values_hbm, *refs):
    count_in = sum(groups)
    pieces, refs = refs[:count_in], refs[count_in:]
    listed, refs = (refs[0], refs[1:]) if only is not None else (None, refs)
    base, refs = (refs[0], refs[1:]) if has_base else (None, refs)
    outs, refs = refs[:count_out], refs[count_out:]
    landed, source, total, values, value_sem, piece_sem, base_sem, out_sem = refs
    count, size = values.shape[0], values.shape[-1]
    halves = source.shape[1]
    width = total.shape[-1] // halves
    each = count // steps
    zero_slot = source.shape[0] - 1

    def value_copy(step):
        part = pl.ds(step * each, each)
        return pltpu.make_async_copy(values_hbm.at[part], values.at[part], value_sem.at[step])

    copies, start = [], 0
    for index, piece in enumerate(pieces):
        part = pl.ds(start, piece.shape[0])
        copies.append(pltpu.make_async_copy(piece, landed.at[part], piece_sem.at[index]))
        start += piece.shape[0]
    if has_base:
        base_copy = pltpu.make_async_copy(base, total, base_sem.at[0])
        base_copy.start()
    for copy in copies:
        copy.start()
    if only is None:
        for step in range(steps):
            value_copy(step).start()
    if not has_base:
        total[...] = jnp.zeros_like(total)

    def slots_of(index):
        row, col = ids[4 + index], ids[4 + count + index]
        if transposed:
            return row_slot(row, ids, per, True), col_slot(col, ids, per)
        return col_slot(col, ids, per), row_slot(row, ids, per, False)

    if only is not None:
        source[zero_slot] = jnp.zeros_like(source[zero_slot])

        found = count - listed[count] if has_base else listed[count]

        def picked(place):
            return listed[count - 1 - place if has_base else place]

        def picked_copy(place):
            return pltpu.make_async_copy(values_hbm.at[picked(place)], values.at[place], value_sem.at[place])

        def start_copy(place, carry):
            picked_copy(place).start()
            return carry

        lax.fori_loop(0, found, start_copy, 0)

    first, slot, start = 0, 0, 0
    for group in groups:
        rows = pieces[first].shape[0]
        for copy in copies[first : first + group]:
            copy.wait()
        for block in range(rows // size):
            terms = [landed[pl.ds(start + m * rows + block * size, size), :] for m in range(group)]
            whole = sum(terms[1:], terms[0])
            for half in range(halves):
                both = jnp.concatenate(two_terms(whole[:, half * width : (half + 1) * width]), axis=1)
                source[slot, half, pl.ds(0, size), :] = both
                source[slot, half, pl.ds(size, size), :] = both
            slot += 1
        first, start = first + group, start + group * rows

    def add_block(place, take, put):
        axis = 0 if transposed else 1
        left = jnp.concatenate(two_terms(values[place]), axis=axis)
        rows = pl.ds(pl.multiple_of(put * size, size), size)
        for half in range(halves):
            product = lax.dot_general(
                left, source[take, half], (((axis,), (0,)), ((), ())), preferred_element_type=jnp.float32
            )
            columns = pl.ds(half * width, width)
            total[rows, columns] += product[:, :width] + product[:, width:]

    if only is None:
        for step in range(steps):
            value_copy(step).wait()

            @pl.loop(0, each // unroll)
            def _(index):
                for k in range(unroll):
                    add_block(step * each + index * unroll + k, *slots_of(step * each + index * unroll + k))

    else:
        if has_base:
            base_copy.wait()

        def add_picked(step, carry):
            for k in range(unroll):
                place = step * unroll + k

                @pl.when(place < found)
                def _():
                    picked_copy(place).wait()

            for k in range(unroll):
                place = step * unroll + k
                inside = place < found
                place = jnp.where(inside, place, 0)
                take, put = slots_of(picked(place))
                add_block(place, jnp.where(inside, take - only[0], zero_slot), put)
            return carry

        lax.fori_loop(0, (found + unroll - 1) // unroll, add_picked, 0)

    copies, start = [], 0
    for index, out in enumerate(outs):
        part = pl.ds(start, out.shape[0])
        copies.append(pltpu.make_async_copy(total.at[part], out, out_sem.at[index]))
        copies[-1].start()
        start += out.shape[0]
    for copy in copies:
        copy.wait()


def list_kernel(slots, per, ids, listed):
    count = listed.shape[0] - 1

    def add(index, found):
        wanted = row_slot(ids[4 + index], ids, per, True) < slots
        listed[jnp.where(wanted, found, count - 1 - index + found)] = index
        return found + wanted.astype(jnp.int32)

    listed[count] = lax.fori_loop(0, count, add, 0)


def list_blocks(ids, count, slots, per):
    smem = pl.BlockSpec(memory_space=pltpu.SMEM)
    return pl.pallas_call(
        functools.partial(list_kernel, slots, per),
        out_shape=jax.ShapeDtypeStruct((count + 1,), jnp.int32),
        in_specs=[smem],
        out_specs=smem,
        compiler_params=pltpu.CompilerParams(vmem_limit_bytes=MIB),
    )(ids)


def spmm(ids, values, groups, out_rows, per, transposed, only=None, listed=None, base=None):
    pieces = [piece for group in groups for piece in group]
    count, size = values.shape[0], values.shape[-1]
    width = pieces[0].shape[1]
    halves = max(1, width // size)
    unroll = next(p for p in ((32, 16, 8, 4, 2, 1) if only is None else (8, 4, 2, 1)) if count % p == 0)
    steps = count // unroll if only is None else 1
    in_rows = sum(group[0].shape[0] for group in groups)
    smem, anywhere = pl.BlockSpec(memory_space=pltpu.SMEM), pl.BlockSpec(memory_space=pl.ANY)
    more = [(smem, listed)] * (only is not None) + [(anywhere, base)] * (base is not None)
    buffers = [
        pltpu.VMEM((sum(piece.shape[0] for piece in pieces), width), jnp.float32),
        pltpu.VMEM((in_rows // size + 1, halves, 2 * size, 2 * (width // halves)), jnp.bfloat16),
        pltpu.VMEM((sum(out_rows), width), jnp.float32),
        pltpu.VMEM(values.shape, jnp.float32),
    ]
    return pl.pallas_call(
        functools.partial(
            spmm_kernel,
            [len(group) for group in groups],
            only,
            base is not None,
            len(out_rows),
            steps,
            unroll,
            per,
            transposed,
        ),
        out_shape=[jax.ShapeDtypeStruct((rows, width), jnp.float32) for rows in out_rows],
        in_specs=[smem] + [anywhere] * (1 + len(pieces)) + [space for space, _ in more],
        out_specs=[anywhere] * len(out_rows),
        scratch_shapes=buffers
        + [
            pltpu.SemaphoreType.DMA((steps if only is None else count,)),
            pltpu.SemaphoreType.DMA((len(pieces),)),
            pltpu.SemaphoreType.DMA((1,)),
            pltpu.SemaphoreType.DMA((len(out_rows),)),
        ],
        compiler_params=pltpu.CompilerParams(
            vmem_limit_bytes=40 * MIB
            if only
            else sum(math.prod(b.shape) * b.dtype.itemsize for b in buffers) + 4 * MIB
        ),
        cost_estimate=pl.CostEstimate(
            flops=8 * count * size * size * width,
            bytes_accessed=4 * (values.size + (in_rows + sum(out_rows)) * width),
            transcendentals=0,
        ),
    )(ids, values, *pieces, *(operand for _, operand in more))


def dense_kernel(count_parts, ids, *refs):
    halves = []
    for half in range(2):
        parts = refs[half * count_parts : (half + 1) * count_parts]
        rows = parts[0][...]
        if count_parts > 1:
            rows = rows + jnp.where(ids[2] != 0, parts[1][...], 0.0)
            for part in parts[2:]:
                rows = rows + part[...]
        halves.append(rows)
    cotangent, weight, hidden, back, grad_out = refs[2 * count_parts :]
    rows = jnp.concatenate(halves, axis=1)
    pre = dot_terms(rows, weight[...], ((1,), (0,)))
    sigmoid_v = 1.0 / (1.0 + jnp.exp(-pre))
    hidden[...] = pre * sigmoid_v
    dpre = cotangent[...] * sigmoid_v * (1.0 + pre * (1.0 - sigmoid_v))
    back[...] = dot_terms(dpre, weight[...], ((1,), (1,)))
    grad_out[...] = dot_terms(rows, dpre, ((0,), (0,)))


def dense(ids, parts, cotangent, weight):
    rows, width = cotangent.shape
    vmem = pl.BlockSpec(memory_space=pltpu.VMEM)
    return pl.pallas_call(
        functools.partial(dense_kernel, len(parts) // 2),
        in_specs=[pl.BlockSpec(memory_space=pltpu.SMEM)] + [vmem] * (len(parts) + 2),
        out_shape=[
            jax.ShapeDtypeStruct((rows, width), jnp.float32),
            jax.ShapeDtypeStruct((rows, width), jnp.float32),
            jax.ShapeDtypeStruct((width, width), jnp.float32),
        ],
        compiler_params=pltpu.CompilerParams(vmem_limit_bytes=20 * MIB),
        cost_estimate=pl.CostEstimate(
            flops=1000,
            bytes_accessed=1000,
            transcendentals=0,
        ),
    )(ids, *parts, cotangent, weight)


def along_row(x, bit):
    return lax.ppermute(x, "row", [(i, i ^ bit) for i in range(lax.axis_size("row"))])


def along_col(x, pairs):
    return lax.ppermute(x, "col", pairs)


def after(x, *others):
    return lax.optimization_barrier((x, *others))[0]


def both_cores(mine, *others):
    return [piece for own in mine for piece in (own, along_row(after(own, *others), 1))]


def plane_exchange(pieces, *others):
    return [pieces[p] + along_row(after(pieces[p + 1], *others), 1) for p in (0, 2, 4, 6)]


def line_reduce(slots, edge, earlier):
    own, outer, across, inner = slots
    outer, middle = after(outer, *earlier), after(inner, *earlier)
    near, middle = along_col(outer, OUTER), along_col(middle, MIDDLE)
    far = along_col(after(across + jnp.where(edge, 0.0, near), middle), ACROSS)
    inward = along_col(after(inner, near, middle), INWARD)
    return [own, near, middle, far, inward]


def core_half(grad):
    upper = lax.axis_index("row") % 2
    rows = grad.shape[0] // 2
    keep = lax.dynamic_slice_in_dim(grad, upper * rows, rows, 0)
    send = lax.dynamic_slice_in_dim(grad, (1 - upper) * rows, rows, 0)
    return keep + along_row(send, 1)


def both_halves(grad):
    other = along_row(grad, 1)
    upper = lax.axis_index("row") % 2
    return jnp.where(upper == 1, jnp.concatenate([other, grad], axis=0), jnp.concatenate([grad, other], axis=0))


def shards(features, weight_matrix, cotangent, block_rows, block_cols, blocks):
    values = blocks[0, 0]
    size = blocks.shape[-1]
    rows_dev, width = features.shape
    per = rows_dev // size
    count_row, count_col = lax.axis_size("row"), lax.axis_size("col")
    total_nodes = rows_dev * count_row * count_col
    me_row, me_col = lax.axis_index("row"), lax.axis_index("col")
    half = width // 2
    features = (features[:, :half], features[:, half:])

    if (count_row, count_col) == (8, 4):
        edge = (me_col == 0) | (me_col == 3)
        place = jnp.stack([me_row, me_col, jnp.where(edge, 2, 0), jnp.where(edge, 0, 3)]).astype(jnp.int32)
        ids = jnp.concatenate([place, block_rows[0, 0], block_cols[0, 0]])
        first, second = features
        diagonal = along_row(first, 6)
        mine = [first, along_row(first, 2), along_row(first, 4), diagonal]
        pieces = both_cores(mine, ids)
        slots = spmm(ids, values, [[p] for p in pieces], [rows_dev] * 4, per, False)
        second = after(second, diagonal)
        mine = [second, along_row(second, 2), along_row(second, 4), along_row(second, 6)]
        terms = line_reduce(slots, edge, [])
        pieces = both_cores(mine, slots[0])
        pieces[0] = after(pieces[0], *terms[1:3])
        slots = spmm(ids, values, [[p] for p in pieces], [rows_dev] * 4, per, False)
        terms += line_reduce(slots, edge, terms[3:5])
        hidden, back, grad = dense(ids, terms, cotangent, weight_matrix)

        ends_across = along_col(back, ENDS_ACROSS)
        listed = list_blocks(after(ids, back), values.shape[0], 2 * per, per)
        later = after(back, ends_across, listed)
        ends_inward, middle = along_col(later, ENDS_INWARD), along_col(later, MIDDLE)
        outward = along_col(ends_across, OUTWARD)
        rest = spmm(ids, values, [[back], [ends_across]], [rows_dev * count_row], per, True, (0, 2 * per), listed)[0]
        grad = core_half(grad)
        grads = [along_row(after(grad, ends_across), bit) for bit in (2, 4, 6)]
        groups = [[after(ends_inward, *grads)], [middle, outward]]
        sums = plane_exchange(
            spmm(ids, values, groups, [rows_dev] * 8, per, True, (2 * per, 4 * per), listed, rest)
        )
        grad = after(grad + grads[0] + grads[1] + grads[2], ends_inward, middle, outward)
        grad = grad + along_col(grad, OUTER)
        upper, lower = sums[3][: rows_dev // 2], sums[3][rows_dev // 2 :]
        upper, lower = after(along_row(upper, 2), grad), along_row(lower, 4)
        others = [
            along_row(sums[1] + jnp.pad(lower, ((rows_dev // 2, 0), (0, 0))), 2),
            along_row(sums[2] + jnp.pad(upper, ((0, rows_dev // 2), (0, 0))), 4),
        ]
        feature_grad = sums[0] + others[0] + others[1]
        grad = both_halves(grad + along_col(grad, ACROSS))
    else:
        place = jnp.zeros((4,), jnp.int32)
        ids = jnp.concatenate([place, block_rows[0, 0], block_cols[0, 0]])
        parts = []
        for own in features:
            gathered = lax.all_gather(own, "row", axis=0, tiled=True)
            (partial,) = spmm(ids, values, [[gathered]], [rows_dev * count_col], per, False)
            parts.append(lax.psum_scatter(partial, "col", scatter_dimension=0, tiled=True))
        hidden, back, grad = dense(ids, parts, cotangent, weight_matrix)
        gathered = lax.all_gather(back, "col", axis=0, tiled=True)
        (partial,) = spmm(ids, values, [[gathered]], [rows_dev * count_row], per, True)
        feature_grad = lax.psum_scatter(partial, "row", scatter_dimension=0, tiled=True)
        grad = lax.psum(grad, ("row", "col"))

    weight_grad = grad / jnp.sqrt(jnp.float32(total_nodes))
    return (hidden, weight_grad, feature_grad)


def solution(mesh):
    in_specs = (
        P(("col", "row"), None),
        P(),
        P(("row", "col"), None),
        P("row", "col", None),
        P("row", "col", None),
        P("row", "col", None, None, None),
    )
    out_specs = (P(("row", "col"), None), P(), P(("col", "row"), None))
    return jax.shard_map(shards, mesh=mesh, in_specs=in_specs, out_specs=out_specs, check_vma=False)
```

```python
import functools
import math

import jax
import jax.numpy as jnp
from jax import lax
from jax.experimental import pallas as pl
from jax.experimental.pallas import tpu as pltpu
from jax.sharding import PartitionSpec as P

MIB = 1024 * 1024

OUTER = ((0, 1), (1, 0), (2, 3), (3, 2))
MIDDLE = ((1, 2), (2, 1))
INWARD = ((0, 1), (3, 2))
OUTWARD = ((1, 0), (2, 3))
ACROSS = ((0, 2), (1, 3), (2, 0), (3, 1))
ENDS_ACROSS = ((0, 2), (3, 1), (1, 0), (2, 3))
ENDS_INWARD = ((2, 0), (1, 3), (0, 1), (3, 2))


def two_terms(x):
    high = x.astype(jnp.bfloat16)
    low = (x - high.astype(jnp.float32)).astype(jnp.bfloat16)
    return high, low


def dot_terms(left, right, dims):
    left_high, left_low = two_terms(left)
    right_high, right_low = two_terms(right)
    dot = functools.partial(
        lax.dot_general, dimension_numbers=(dims, ((), ())), preferred_element_type=jnp.float32
    )
    return dot(left_high, right_high) + (dot(left_high, right_low) + dot(left_low, right_high))


def split_index(block, per):
    if per & (per - 1) == 0:
        return block >> (per.bit_length() - 1), block & (per - 1)
    return block // per, block % per


def row_slot(block, place, per, gathered):
    chunk, inside = split_index(block, per)
    group = chunk ^ place[1]
    if gathered:
        group = group ^ (place[3] * ((group ^ (group >> 1)) & 1))
    else:
        group = group ^ (place[2] * (group & 1))
    return group * per + inside


def col_slot(block, place, per):
    chunk, inside = split_index(block, per)
    return (chunk ^ place[0]) * per + inside


def spmm_kernel(groups, only, has_base, count_out, steps, unroll, per, transposed, ids, values_hbm, *refs):
    count_in = sum(groups)
    pieces, refs = refs[:count_in], refs[count_in:]
    listed, refs = (refs[0], refs[1:]) if only is not None else (None, refs)
    base, refs = (refs[0], refs[1:]) if has_base else (None, refs)
    outs, refs = refs[:count_out], refs[count_out:]
    landed, source, total, values, value_sem, piece_sem, base_sem, out_sem = refs
    count, size = values.shape[0], values.shape[-1]
    halves = source.shape[1]
    width = total.shape[-1] // halves
    each = count // steps
    zero_slot = source.shape[0] - 1

    def value_copy(step):
        part = pl.ds(step * each, each)
        return pltpu.make_async_copy(values_hbm.at[part], values.at[part], value_sem.at[step])

    copies, start = [], 0
    for index, piece in enumerate(pieces):
        part = pl.ds(start, piece.shape[0])
        copies.append(pltpu.make_async_copy(piece, landed.at[part], piece_sem.at[index]))
        start += piece.shape[0]
    if has_base:
        base_copy = pltpu.make_async_copy(base, total, base_sem.at[0])
        base_copy.start()
    for copy in copies:
        copy.start()
    if only is None:
        for step in range(steps):
            value_copy(step).start()
    if not has_base:
        total[...] = jnp.zeros_like(total)

    def slots_of(index):
        row, col = ids[4 + index], ids[4 + count + index]
        if transposed:
            return row_slot(row, ids, per, True), col_slot(col, ids, per)
        return col_slot(col, ids, per), row_slot(row, ids, per, False)

    if only is not None:
        source[zero_slot] = jnp.zeros_like(source[zero_slot])

        found = count - listed[count] if has_base else listed[count]

        def picked(place):
            return listed[count - 1 - place if has_base else place]

        def picked_copy(place):
            return pltpu.make_async_copy(values_hbm.at[picked(place)], values.at[place], value_sem.at[place])

        def start_copy(place, carry):
            picked_copy(place).start()
            return carry

        lax.fori_loop(0, found, start_copy, 0)

    first, slot, start = 0, 0, 0
    for group in groups:
        rows = pieces[first].shape[0]
        for copy in copies[first : first + group]:
            copy.wait()
        for block in range(rows // size):
            terms = [landed[pl.ds(start + m * rows + block * size, size), :] for m in range(group)]
            whole = sum(terms[1:], terms[0])
            for half in range(halves):
                both = jnp.concatenate(two_terms(whole[:, half * width : (half + 1) * width]), axis=1)
                source[slot, half, pl.ds(0, size), :] = both
                source[slot, half, pl.ds(size, size), :] = both
            slot += 1
        first, start = first + group, start + group * rows

    def add_block(place, take, put):
        axis = 0 if transposed else 1
        left = jnp.concatenate(two_terms(values[place]), axis=axis)
        rows = pl.ds(pl.multiple_of(put * size, size), size)
        for half in range(halves):
            product = lax.dot_general(
                left, source[take, half], (((axis,), (0,)), ((), ())), preferred_element_type=jnp.float32
            )
            columns = pl.ds(half * width, width)
            total[rows, columns] += product[:, :width] + product[:, width:]

    if only is None:
        for step in range(steps):
            value_copy(step).wait()

            @pl.loop(0, each // unroll)
            def _(index):
                for k in range(unroll):
                    add_block(step * each + index * unroll + k, *slots_of(step * each + index * unroll + k))

    else:
        if has_base:
            base_copy.wait()

        def add_picked(step, carry):
            for k in range(unroll):
                place = step * unroll + k

                @pl.when(place < found)
                def _():
                    picked_copy(place).wait()

            for k in range(unroll):
                place = step * unroll + k
                inside = place < found
                place = jnp.where(inside, place, 0)
                take, put = slots_of(picked(place))
                add_block(place, jnp.where(inside, take - only[0], zero_slot), put)
            return carry

        lax.fori_loop(0, (found + unroll - 1) // unroll, add_picked, 0)

    copies, start = [], 0
    for index, out in enumerate(outs):
        part = pl.ds(start, out.shape[0])
        copies.append(pltpu.make_async_copy(total.at[part], out, out_sem.at[index]))
        copies[-1].start()
        start += out.shape[0]
    for copy in copies:
        copy.wait()


def list_kernel(slots, per, ids, listed):
    count = listed.shape[0] - 1

    def add(index, found):
        wanted = row_slot(ids[4 + index], ids, per, True) < slots
        listed[jnp.where(wanted, found, count - 1 - index + found)] = index
        return found + wanted.astype(jnp.int32)

    listed[count] = lax.fori_loop(0, count, add, 0)


def list_blocks(ids, count, slots, per):
    smem = pl.BlockSpec(memory_space=pltpu.SMEM)
    return pl.pallas_call(
        functools.partial(list_kernel, slots, per),
        out_shape=jax.ShapeDtypeStruct((count + 1,), jnp.int32),
        in_specs=[smem],
        out_specs=smem,
        compiler_params=pltpu.CompilerParams(vmem_limit_bytes=MIB),
    )(ids)


def spmm(ids, values, groups, out_rows, per, transposed, only=None, listed=None, base=None):
    pieces = [piece for group in groups for piece in group]
    count, size = values.shape[0], values.shape[-1]
    width = pieces[0].shape[1]
    halves = max(1, width // size)
    unroll = next(p for p in ((32, 16, 8, 4, 2, 1) if only is None else (16, 8, 4, 2, 1)) if count % p == 0)
    steps = count // unroll if only is None else 1
    in_rows = sum(group[0].shape[0] for group in groups)
    smem, anywhere = pl.BlockSpec(memory_space=pltpu.SMEM), pl.BlockSpec(memory_space=pl.ANY)
    more = [(smem, listed)] * (only is not None) + [(anywhere, base)] * (base is not None)
    buffers = [
        pltpu.VMEM((sum(piece.shape[0] for piece in pieces), width), jnp.float32),
        pltpu.VMEM((in_rows // size + 1, halves, 2 * size, 2 * (width // halves)), jnp.bfloat16),
        pltpu.VMEM((sum(out_rows), width), jnp.float32),
        pltpu.VMEM(values.shape, jnp.float32),
    ]
    return pl.pallas_call(
        functools.partial(
            spmm_kernel,
            [len(group) for group in groups],
            only,
            base is not None,
            len(out_rows),
            steps,
            unroll,
            per,
            transposed,
        ),
        out_shape=[jax.ShapeDtypeStruct((rows, width), jnp.float32) for rows in out_rows],
        in_specs=[smem] + [anywhere] * (1 + len(pieces)) + [space for space, _ in more],
        out_specs=[anywhere] * len(out_rows),
        scratch_shapes=buffers
        + [
            pltpu.SemaphoreType.DMA((steps if only is None else count,)),
            pltpu.SemaphoreType.DMA((len(pieces),)),
            pltpu.SemaphoreType.DMA((1,)),
            pltpu.SemaphoreType.DMA((len(out_rows),)),
        ],
        compiler_params=pltpu.CompilerParams(
            vmem_limit_bytes=40 * MIB
            if only
            else sum(math.prod(b.shape) * b.dtype.itemsize for b in buffers) + 4 * MIB
        ),
        cost_estimate=pl.CostEstimate(
            flops=8 * count * size * size * width,
            bytes_accessed=4 * (values.size + (in_rows + sum(out_rows)) * width),
            transcendentals=0,
        ),
    )(ids, values, *pieces, *(operand for _, operand in more))


def dense_kernel(count_parts, ids, *refs):
    halves = []
    for half in range(2):
        parts = refs[half * count_parts : (half + 1) * count_parts]
        rows = parts[0][...]
        if count_parts > 1:
            rows = rows + jnp.where(ids[2] != 0, parts[1][...], 0.0)
            for part in parts[2:]:
                rows = rows + part[...]
        halves.append(rows)
    cotangent, weight, hidden, back, grad_out = refs[2 * count_parts :]
    rows = jnp.concatenate(halves, axis=1)
    pre = dot_terms(rows, weight[...], ((1,), (0,)))
    sigmoid_v = 1.0 / (1.0 + jnp.exp(-pre))
    hidden[...] = pre * sigmoid_v
    dpre = cotangent[...] * sigmoid_v * (1.0 + pre * (1.0 - sigmoid_v))
    back[...] = dot_terms(dpre, weight[...], ((1,), (1,)))
    grad_out[...] = dot_terms(rows, dpre, ((0,), (0,)))


def dense(ids, parts, cotangent, weight):
    rows, width = cotangent.shape
    vmem = pl.BlockSpec(memory_space=pltpu.VMEM)
    return pl.pallas_call(
        functools.partial(dense_kernel, len(parts) // 2),
        in_specs=[pl.BlockSpec(memory_space=pltpu.SMEM)] + [vmem] * (len(parts) + 2),
        out_shape=[
            jax.ShapeDtypeStruct((rows, width), jnp.float32),
            jax.ShapeDtypeStruct((rows, width), jnp.float32),
            jax.ShapeDtypeStruct((width, width), jnp.float32),
        ],
        compiler_params=pltpu.CompilerParams(vmem_limit_bytes=20 * MIB),
        cost_estimate=pl.CostEstimate(
            flops=1000,
            bytes_accessed=1000,
            transcendentals=0,
        ),
    )(ids, *parts, cotangent, weight)


def along_row(x, bit):
    return lax.ppermute(x, "row", [(i, i ^ bit) for i in range(lax.axis_size("row"))])


def along_col(x, pairs):
    return lax.ppermute(x, "col", pairs)


def after(x, *others):
    return lax.optimization_barrier((x, *others))[0]


def both_cores(mine, *others):
    return [piece for own in mine for piece in (own, along_row(after(own, *others), 1))]


def plane_exchange(pieces, *others):
    return [pieces[p] + along_row(after(pieces[p + 1], *others), 1) for p in (0, 2, 4, 6)]


def line_reduce(slots, edge, earlier):
    own, outer, across, inner = slots
    outer, middle = after(outer, *earlier), after(inner, *earlier)
    near, middle = along_col(outer, OUTER), along_col(middle, MIDDLE)
    far = along_col(after(across + jnp.where(edge, 0.0, near), middle), ACROSS)
    inward = along_col(after(inner, near, middle), INWARD)
    return [own, near, middle, far, inward]


def core_half(grad):
    upper = lax.axis_index("row") % 2
    rows = grad.shape[0] // 2
    keep = lax.dynamic_slice_in_dim(grad, upper * rows, rows, 0)
    send = lax.dynamic_slice_in_dim(grad, (1 - upper) * rows, rows, 0)
    return keep + along_row(send, 1)


def both_halves(grad):
    other = along_row(grad, 1)
    upper = lax.axis_index("row") % 2
    return jnp.where(upper == 1, jnp.concatenate([other, grad], axis=0), jnp.concatenate([grad, other], axis=0))


def shards(features, weight_matrix, cotangent, block_rows, block_cols, blocks):
    values = blocks[0, 0]
    size = blocks.shape[-1]
    rows_dev, width = features.shape
    per = rows_dev // size
    count_row, count_col = lax.axis_size("row"), lax.axis_size("col")
    total_nodes = rows_dev * count_row * count_col
    me_row, me_col = lax.axis_index("row"), lax.axis_index("col")
    half = width // 2
    features = (features[:, :half], features[:, half:])

    if (count_row, count_col) == (8, 4):
        edge = (me_col == 0) | (me_col == 3)
        place = jnp.stack([me_row, me_col, jnp.where(edge, 2, 0), jnp.where(edge, 0, 3)]).astype(jnp.int32)
        ids = jnp.concatenate([place, block_rows[0, 0], block_cols[0, 0]])
        first, second = features
        diagonal = along_row(first, 6)
        mine = [first, along_row(first, 2), along_row(first, 4), diagonal]
        pieces = both_cores(mine, ids)
        slots = spmm(ids, values, [[p] for p in pieces], [rows_dev] * 4, per, False)
        second = after(second, diagonal)
        mine = [second, along_row(second, 2), along_row(second, 4), along_row(second, 6)]
        terms = line_reduce(slots, edge, [])
        pieces = both_cores(mine, slots[0])
        pieces[0] = after(pieces[0], *terms[1:3])
        slots = spmm(ids, values, [[p] for p in pieces], [rows_dev] * 4, per, False)
        terms += line_reduce(slots, edge, terms[3:5])
        hidden, back, grad = dense(ids, terms, cotangent, weight_matrix)

        ends_across = along_col(back, ENDS_ACROSS)
        listed = list_blocks(after(ids, back), values.shape[0], 2 * per, per)
        later = after(back, ends_across, listed)
        ends_inward, middle = along_col(later, ENDS_INWARD), along_col(later, MIDDLE)
        outward = along_col(ends_across, OUTWARD)
        rest = spmm(ids, values, [[back], [ends_across]], [rows_dev * count_row], per, True, (0, 2 * per), listed)[0]
        grad = core_half(grad)
        grads = [along_row(after(grad, ends_across), bit) for bit in (2, 4, 6)]
        groups = [[after(ends_inward, *grads)], [middle, outward]]
        sums = plane_exchange(
            spmm(ids, values, groups, [rows_dev] * 8, per, True, (2 * per, 4 * per), listed, rest)
        )
        grad = after(grad + grads[0] + grads[1] + grads[2], ends_inward, middle, outward)
        grad = grad + along_col(grad, OUTER)
        upper, lower = sums[3][: rows_dev // 2], sums[3][rows_dev // 2 :]
        upper, lower = after(along_row(upper, 2), grad), along_row(lower, 4)
        others = [
            along_row(sums[1] + jnp.pad(lower, ((rows_dev // 2, 0), (0, 0))), 2),
            along_row(sums[2] + jnp.pad(upper, ((0, rows_dev // 2), (0, 0))), 4),
        ]
        feature_grad = sums[0] + others[0] + others[1]
        grad = both_halves(grad + along_col(grad, ACROSS))
    else:
        place = jnp.zeros((4,), jnp.int32)
        ids = jnp.concatenate([place, block_rows[0, 0], block_cols[0, 0]])
        parts = []
        for own in features:
            gathered = lax.all_gather(own, "row", axis=0, tiled=True)
            (partial,) = spmm(ids, values, [[gathered]], [rows_dev * count_col], per, False)
            parts.append(lax.psum_scatter(partial, "col", scatter_dimension=0, tiled=True))
        hidden, back, grad = dense(ids, parts, cotangent, weight_matrix)
        gathered = lax.all_gather(back, "col", axis=0, tiled=True)
        (partial,) = spmm(ids, values, [[gathered]], [rows_dev * count_row], per, True)
        feature_grad = lax.psum_scatter(partial, "row", scatter_dimension=0, tiled=True)
        grad = lax.psum(grad, ("row", "col"))

    weight_grad = grad / jnp.sqrt(jnp.float32(total_nodes))
    return (hidden, weight_grad, feature_grad)


def solution(mesh):
    in_specs = (
        P(("col", "row"), None),
        P(),
        P(("row", "col"), None),
        P("row", "col", None),
        P("row", "col", None),
        P("row", "col", None, None, None),
    )
    out_specs = (P(("row", "col"), None), P(), P(("col", "row"), None))
    return jax.shard_map(shards, mesh=mesh, in_specs=in_specs, out_specs=out_specs, check_vma=False)
```
